32 devices in a mesh: grp: 4 (over y, x), patch: 8 (over z, core).
Axes of the slice: x: 2, y: 2, z: 4, core: 2. Of those that a mesh axis runs over, the one named last changes fastest.
Arguments:
- fine_latent: bfloat16 [4096, 512], P(('grp', 'patch')), may hold values from -6 to 6
- edge_latent: bfloat16 [16384, 512], P(('grp', 'patch')), may hold values from -13 to 13
- coarse_latent: bfloat16 [256, 512], replicated, may hold values from -6 to 6
- first_proj: bfloat16 [1536, 512], P('patch'), may hold values from -0.15625 to 0.15625
- second_proj: bfloat16 [512, 512], P('patch'), may hold values from -1 to 1
- senders: int32 [16384], P(('grp', 'patch')), may hold values from 0 to 511, as said below
- receivers: int32 [16384], P(('grp', 'patch')), may hold values from 0 to 127
- block_counts: int32 [128], P(('grp', 'patch')), may hold values from 64 to 128, as said below
- send_rows: int32 [128, 32], P(('grp', 'patch')), may hold values from 0 to 127, as said below
- cot_edges: bfloat16 [16384, 512], P(('grp', 'patch')), may hold values from -6 to 6
- cot_fine: bfloat16 [4096, 512], P(('grp', 'patch')), may hold values from -6 to 6
Outputs:
- new_edges: bfloat16 [16384, 512], P(('grp', 'patch'))
- fine_messages: bfloat16 [4096, 512], P(('grp', 'patch'))
- grad_edges: bfloat16 [16384, 512], P(('grp', 'patch'))
- grad_fine: bfloat16 [4096, 512], P(('grp', 'patch'))
- grad_coarse: float32 [256, 512], P('patch')
- grad_first: float32 [1536, 512], P('patch')
- grad_second: float32 [512, 512], P('patch')
The draws below stay inside these ranges and needn't reach their ends.
Inputs may be any that keep to these rules, and one draw needn't show every extreme that they name: `senders`: A sender below 128 is a local fine node, the next 128 rows are the received rows in the table's order, the last 256 are coarse nodes. `block_counts`: the live edges of a block of 128 slots are its first ones; some block holds 128 and some 64. `send_rows`: each list holds 32 distinct local rows.
All inputs are finite; a program needn't handle non-finite values.
Results may differ from the reference program's by a relative error of at most 0.015.
Values may be sent and summed in bfloat16 or wider, within the bound.
A program may use at most 64 MiB of HBM per device.

```python
import math
import jax
import jax.numpy as jnp
from jax import lax

D = 512
NF_DEV = 128
E_DEV = 512
NC = 256
H = 32
LAT = 4
LON = 8
NODES = 4096
EDGES = 16384
BLOCKS = 128
LISTS = 128


def draw_senders(key, part):
    key = jax.random.fold_in(key, 11)
    key_kind, key_local, key_halo, key_coarse = jax.random.split(key, 4)
    kind = jax.random.randint(key_kind, (EDGES,), 0, 8)
    local = jax.random.randint(key_local, (EDGES,), 0, NF_DEV)
    halo = NF_DEV + jax.random.randint(key_halo, (EDGES,), 0, 4 * H)
    coarse = NF_DEV + 4 * H + jax.random.randint(key_coarse, (EDGES,), 0, NC)
    return jnp.where(kind < 3, local, jnp.where(kind < 5, halo, coarse)).astype(jnp.int32)


def draw_block_counts(key, part):
    key = jax.random.fold_in(key, 12)
    key_count, key_full, key_empty = jax.random.split(key, 3)
    counts = jax.random.randint(key_count, (BLOCKS,), 64, 129)
    fullest = jax.random.randint(key_full, (), 0, BLOCKS)
    emptiest = jax.random.randint(key_empty, (), 0, BLOCKS)
    counts = counts.at[emptiest].set(64).at[fullest].set(128)
    return counts.astype(jnp.int32)


def draw_send_rows(key, part):
    key = jax.random.fold_in(key, 13)
    keys = jax.random.split(key, LISTS)
    orders = jax.vmap(lambda one_key: jax.random.permutation(one_key, NF_DEV))(keys)
    return orders[:, :H].astype(jnp.int32)


def draw_edge_latent(key, part):
    key = jax.random.fold_in(key, 14)
    key_base, key_scale = jax.random.split(key, 2)
    base = jnp.clip(jax.random.normal(key_base, (EDGES, D), jnp.float32), -4.0, 4.0)
    scales = jnp.exp(jax.random.uniform(key_scale, (EDGES, 1), jnp.float32, -1.15, 1.15))
    return (base * scales).astype(jnp.bfloat16)


def draw_second_proj(key, part):
    key = jax.random.fold_in(key, 15)
    key_base, key_scale = jax.random.split(key, 2)
    base = jnp.clip(jax.random.normal(key_base, (D, D), jnp.float32), -2.5, 2.5)
    scales = jnp.exp(jax.random.uniform(key_scale, (1, D), jnp.float32, -1.15, 1.15))
    return (base * scales / math.sqrt(D)).astype(jnp.bfloat16)


def place_ends(entries, stream_key, low, largest):
    longest = entries.shape.index(max(entries.shape))
    spots = []
    for shift in (0, 1):
        where = [jax.random.randint(jax.random.fold_in(stream_key, axis), (), 0, length) for axis, length in enumerate(entries.shape)]
        where[longest] = (where[longest] + shift) % entries.shape[longest]
        spots.append(tuple(where))
    return entries.at[spots[0]].set(low).at[spots[1]].set(largest)


def shard_levels(rng, dims, cuts, least, largest):
    factor_of, own = 1.0, jax.random.fold_in(rng, 6)
    for axis_at, blocks in cuts:
        heights = jnp.exp(jax.random.uniform(jax.random.fold_in(own, axis_at), (blocks,), jnp.float32, least / len(cuts), largest / len(cuts)))
        factor_of = factor_of * jnp.repeat(heights, dims[axis_at] // blocks).reshape([-1 if axis == axis_at else 1 for axis in range(len(dims))])
    return factor_of


def normal_values(own_key, shape, scale, most, pieces=(), held_as=jnp.bfloat16):
    array = jax.random.normal(own_key, shape, jnp.float32) * scale
    if len(pieces) > 0:
        array = shard_levels(own_key, shape, pieces, -0.22, 0.18) * array
    return jnp.clip(array, min=-most, max=most).astype(held_as)


def setup_inputs(seed: int = 0) -> dict:
    splits = jax.random.split(jax.random.key(seed), 12)
    return {
        "fine_latent": normal_values(splits[0], (NODES, D), 1.0, 6.0, ((0, 32),)),
        "edge_latent": draw_edge_latent(jax.random.fold_in(splits[11], 71), 0),
        "coarse_latent": normal_values(splits[2], (NC, D), 1.0, 6.0),
        "first_proj": normal_values(splits[3], (3 * D, D), (3 * D) ** -0.5, 0.15625, ((0, 8),)),
        "second_proj": draw_second_proj(jax.random.fold_in(splits[11], 71), 0),
        "senders": draw_senders(jax.random.fold_in(splits[11], 71), 0),
        "receivers": place_ends(jax.random.randint(splits[6], (EDGES,), 0, NF_DEV), jax.random.fold_in(splits[6], 1), 0, NF_DEV - 1).astype(jnp.int32),
        "block_counts": draw_block_counts(jax.random.fold_in(splits[11], 71), 0),
        "send_rows": draw_send_rows(jax.random.fold_in(splits[11], 71), 0),
        "cot_edges": normal_values(splits[9], (EDGES, D), 1.0, 6.0, ((0, 32),)),
        "cot_fine": normal_values(splits[10], (NODES, D), 1.0, 6.0, ((0, 32),)),
    }


norm_eps = 1e-05

def edge_pass(fine_rows, halo_rows, coarse_latent, first_proj, second_proj, edge_rows, senders, receivers, counts, cot_edge, cot_node):
    node_count = fine_rows.shape[0]
    halo_count = halo_rows.shape[0]
    node_table = jnp.concatenate([fine_rows, halo_rows, coarse_latent], axis=0)
    positions = jnp.arange(128).astype(jnp.int32)
    live_mask = (positions[None, :] < counts[:, None]).reshape(-1).astype(jnp.float32)[:, None]
    joined = jnp.concatenate([edge_rows, node_table[senders], fine_rows[receivers]], axis=1)
    pre_act = jnp.dot(joined, first_proj, preferred_element_type=jnp.float32)
    hidden = jax.nn.silu(pre_act).astype(jnp.bfloat16)
    outer_proj = jnp.dot(hidden, second_proj, preferred_element_type=jnp.float32)
    centre = outer_proj - lax.optimization_barrier(jnp.mean(outer_proj, axis=1, keepdims=True))
    norm_scale = jnp.sqrt(lax.optimization_barrier(jnp.mean(centre * centre, axis=1, keepdims=True)) + norm_eps)
    normed = centre / norm_scale
    message = live_mask * normed
    new_edges = (edge_rows.astype(jnp.float32) + message).astype(jnp.bfloat16)
    fine_messages = jax.ops.segment_sum(message, receivers, num_segments=node_count).astype(jnp.bfloat16)
    upstream = live_mask * (cot_edge.astype(jnp.float32) + cot_node[receivers].astype(jnp.float32))
    d_outer = ((upstream - lax.optimization_barrier(jnp.mean(upstream, axis=1, keepdims=True)) - normed * lax.optimization_barrier(jnp.mean(upstream * normed, axis=1, keepdims=True))) / norm_scale).astype(jnp.bfloat16)
    d_hidden = jnp.dot(d_outer, second_proj.T, preferred_element_type=jnp.float32)
    gate_sig = jax.nn.sigmoid(pre_act)
    d_pre = (d_hidden * gate_sig * (1.0 + pre_act * (1.0 - gate_sig))).astype(jnp.bfloat16)
    d_joined = jnp.dot(d_pre, first_proj.T, preferred_element_type=jnp.float32)
    grad_edges = (cot_edge.astype(jnp.float32) + d_joined[:, :D]).astype(jnp.bfloat16)
    d_table = jax.ops.segment_sum(d_joined[:, D:2 * D], senders, num_segments=node_table.shape[0])
    local_grad = d_table[:node_count] + jax.ops.segment_sum(d_joined[:, 2 * D:], receivers, num_segments=node_count)
    halo_back = d_table[node_count:node_count + halo_count].astype(jnp.bfloat16)
    coarse_part = d_table[node_count + halo_count:]
    first_part = jnp.dot(joined.T, d_pre, preferred_element_type=jnp.float32).astype(jnp.bfloat16)
    second_part = jnp.dot(hidden.T, d_outer, preferred_element_type=jnp.float32).astype(jnp.bfloat16)
    return (new_edges, fine_messages, grad_edges, local_grad, halo_back, coarse_part, first_part, second_part)

def swap_blocks(blocks):
    return jnp.stack([jnp.roll(blocks[:, :, 1], 1, axis=1), jnp.roll(blocks[:, :, 0], -1, axis=1), jnp.roll(blocks[:, :, 3], 1, axis=0), jnp.roll(blocks[:, :, 2], -1, axis=0)], axis=2)

def reference(fine_latent, edge_latent, coarse_latent, first_proj, second_proj, senders, receivers, block_counts, send_rows, cot_edges, cot_fine):
    patches = LAT * LON
    patch_grid = fine_latent.reshape(LAT, LON, NF_DEV, D)
    send_lists = send_rows.reshape(LAT, LON, 4, H)
    outgoing = jax.vmap(jax.vmap(lambda latent, picks: latent[picks]))(patch_grid, send_lists)
    halo_rows = swap_blocks(outgoing).reshape(patches, 4 * H, D)

    def visit_patch(totals, per_patch):
        fine_rows, halo_part, edge_rows, send_part, recv_part, count_part, cot_edge, cot_node = per_patch
        results = edge_pass(fine_rows, halo_part, coarse_latent, first_proj, second_proj, edge_rows, send_part, recv_part, count_part, cot_edge, cot_node)
        new_edges, fine_msg, grad_edges, local_grad, halo_back, coarse_part, first_part, second_part = results
        totals = (totals[0] + first_part.astype(jnp.float32), totals[1] + second_part.astype(jnp.float32), totals[2] + coarse_part)
        return (totals, (new_edges, fine_msg, grad_edges, local_grad, halo_back))
    initial = (jnp.zeros((3 * D, D), jnp.float32), jnp.zeros((D, D), jnp.float32), jnp.zeros((NC, D), jnp.float32))
    per_patch = (fine_latent.reshape(patches, NF_DEV, D), halo_rows, edge_latent.reshape(patches, E_DEV, D), senders.reshape(patches, E_DEV), receivers.reshape(patches, E_DEV), block_counts.reshape(patches, E_DEV // 128), cot_edges.reshape(patches, E_DEV, D), cot_fine.reshape(patches, NF_DEV, D))
    totals, outputs = lax.scan(visit_patch, initial, per_patch)
    new_edges, fine_messages, grad_edges, local_grad, halo_back = outputs
    returned = swap_blocks(halo_back.reshape(LAT, LON, 4, H, D)).reshape(patches, 4 * H, D).astype(jnp.float32)
    added = jax.vmap(lambda grads, picks: jax.ops.segment_sum(grads, picks, num_segments=NF_DEV))(returned, send_rows.reshape(patches, 4 * H))
    grad_fine = (local_grad + added).astype(jnp.bfloat16).reshape(NODES, D)
    return (new_edges.reshape(EDGES, D), fine_messages.reshape(NODES, D), grad_edges.reshape(EDGES, D), grad_fine, totals[2], totals[0], totals[1])
```

```python
import functools

import jax
import jax.numpy as jnp
from jax import lax
from jax.experimental import pallas as pl
from jax.experimental.pallas import tpu as pltpu
from jax.sharding import PartitionSpec as P

norm_eps = 1e-05
LANES = 128
ROW_TILE = 16
EDGE_BLOCK = 256
PART_ROWS = 384
F32 = jnp.float32
BF16 = jnp.bfloat16


def dot(x, y):
    return jnp.dot(x, y, preferred_element_type=F32)


def dot_nt(x, y):
    return lax.dot_general(x, y, (((1,), (1,)), ((), ())), preferred_element_type=F32)


def dot_tn(x, y):
    return lax.dot_general(x, y, (((0,), (0,)), ((), ())), preferred_element_type=F32)


def picks(rows, index_row):
    where = lax.broadcasted_iota(jnp.int32, (rows, index_row.shape[1]), 0)
    return (where == index_row).astype(F32).astype(BF16)


def row_mean(x):
    return jnp.mean(x, axis=1, keepdims=True)


def kernel(
    groups,
    patches,
    counts_ref,
    fine_ref,
    edge_ref,
    coarse_ref,
    first_ref,
    second_ref,
    send_idx_ref,
    recv_idx_ref,
    list_idx_ref,
    cot_edge_ref,
    cot_fine_ref,
    new_edges_ref,
    fine_msg_ref,
    grad_edges_ref,
    grad_fine_ref,
    grad_coarse_ref,
    grad_first_ref,
    grad_second_ref,
    weights,
    outgoing,
    table,
    pick_send,
    pick_recv,
    joined,
    hidden,
    d_outer_all,
    d_pre_all,
    message_all,
    d_send_all,
    d_recv_all,
    halo_back,
    returned,
    parts,
    from_core,
    chip_sum,
    from_grp,
    plane_sum,
    from_z,
    whole_sum,
    from_far,
    result,
    w_z_sems,
    w_grp_sems,
    w_core_sems,
    halo_sems,
    back_sems,
    core_sems,
    grp_sems,
    z_sems,
    far_sems,
    result_sems,
):
    a = lax.axis_index("grp")
    b = lax.axis_index("patch")
    z = b // 2
    c = b % 2
    chips = patches // 2
    width = fine_ref.shape[1]
    blocks = width // LANES
    k = a % blocks
    base = a - k
    far_count = groups // blocks
    first_rows = first_ref.shape[0]
    second_rows = second_ref.shape[0]
    coarse_rows = grad_coarse_ref.shape[0]
    node_count = fine_ref.shape[0]
    halo_count = list_idx_ref.shape[1]
    list_rows = halo_count // 4
    edge_count = edge_ref.shape[0]
    weight_rows = first_rows + second_rows
    part_rows = parts.shape[1]
    sibling = (a, 2 * z + 1 - c)
    pending = []

    def send(src, dst, sems, at, device):
        copy = pltpu.make_async_remote_copy(
            src_ref=src,
            dst_ref=dst,
            send_sem=sems.at[(0,) + at],
            recv_sem=sems.at[(1,) + at],
            device_id=device,
            device_id_type=pl.DeviceIdType.MESH,
        )
        copy.start()
        pending.append(copy)
        return copy

    def columns(block):
        return pl.ds(pl.multiple_of(block * LANES, LANES), LANES)

    def chip_at(offset):
        return (z + offset + chips) % chips

    def peer(offset):
        return (base + (k + offset) % blocks, b)

    def exchange(src, dst, first_row, sems):
        routes = (
            (1, 0, (a, (b + 1) % patches)),
            (0, 1, (a, (b + patches - 1) % patches)),
            (3, 2, ((a + 1) % groups, b)),
            (2, 3, ((a + groups - 1) % groups, b)),
        )
        return [
            send(
                src.at[pl.ds(own * list_rows, list_rows), :],
                dst.at[pl.ds(first_row + slot * list_rows, list_rows), :],
                sems,
                (slot,),
                device,
            )
            for own, slot, device in routes
        ]

    barrier = pltpu.get_barrier_semaphore()
    for step in range(1, patches):
        pl.semaphore_signal(
            barrier, inc=1, device_id=(a, (b + step) % patches), device_id_type=pl.DeviceIdType.MESH
        )
    for step in range(1, groups):
        pl.semaphore_signal(
            barrier, inc=1, device_id=((a + step) % groups, b), device_id_type=pl.DeviceIdType.MESH
        )
    weights[b, :first_rows, :] = first_ref[...]
    weights[b, first_rows:, :] = second_ref[...]
    pick_list = picks(node_count, list_idx_ref[...])
    outgoing[...] = dot_tn(pick_list, fine_ref[...]).astype(BF16)
    pl.semaphore_wait(barrier, patches + groups - 2)

    along_z = [
        send(
            weights.at[b, :, columns(k)],
            weights.at[b, :, columns(k)],
            w_z_sems,
            (step - 1,),
            (a, 2 * chip_at(step) + c),
        )
        for step in range(1, chips)
    ]
    between = [send(weights.at[b], weights.at[b], w_core_sems, (0,), sibling)]
    halo = exchange(outgoing, table, node_count, halo_sems)
    table[:node_count, :] = fine_ref[...]
    table[node_count + halo_count :, :] = coarse_ref[...]
    over_grp = []
    for step in range(1, chips):
        along_z[step - 1].wait_recv()
        owner = 2 * chip_at(-step) + c
        over_grp.append(
            [
                send(
                    weights.at[owner, :, columns(k)],
                    weights.at[owner, :, columns(k)],
                    w_grp_sems,
                    (step - 1, offset - 1),
                    peer(offset),
                )
                for offset in range(1, blocks)
            ]
        )
    pick_send[...] = picks(table.shape[0], send_idx_ref[...])
    pick_recv[...] = picks(node_count, recv_idx_ref[...])
    joined[:, :width] = edge_ref[...]
    joined[:, 2 * width :] = dot_tn(pick_recv[...], fine_ref[...]).astype(BF16)
    for step in range(1, chips):
        for copy in over_grp[step - 1]:
            copy.wait_recv()
        owner = 2 * chip_at(-step) + c
        between.append(
            send(weights.at[owner], weights.at[owner], w_core_sems, (step,), sibling)
        )
    for copy in halo:
        copy.wait_recv()
    joined[:, width : 2 * width] = dot_tn(pick_send[...], table[...]).astype(BF16)
    for copy in between:
        copy.wait_recv()

    @pl.loop(0, edge_count // EDGE_BLOCK)
    def _(at):
        rows = pl.ds(pl.multiple_of(at * EDGE_BLOCK, EDGE_BLOCK), EDGE_BLOCK)
        first_full = weights[:, :first_rows, :].reshape(patches * first_rows, width)
        second_full = weights[:, first_rows:, :].reshape(patches * second_rows, width)
        pre_act = dot(joined[rows, :], first_full)
        gate_sig = 1.0 / (1.0 + jnp.exp(-pre_act))
        hid = (pre_act * gate_sig).astype(BF16)
        hidden[rows, :] = hid
        outer_proj = dot(hid, second_full)
        centre = outer_proj - row_mean(outer_proj)
        inv_scale = 1.0 / jnp.sqrt(row_mean(centre * centre) + norm_eps)
        normed = centre * inv_scale
        position = lax.broadcasted_iota(jnp.int32, (EDGE_BLOCK, 1), 0)
        per = EDGE_BLOCK // LANES
        bound = counts_ref[at * per]
        for extra in range(1, per):
            bound = jnp.where(
                position < extra * LANES, bound, counts_ref[at * per + extra] + extra * LANES
            )
        live = (position < bound).astype(F32)
        message = live * normed
        message_all[rows, :] = message.astype(BF16)
        new_edges_ref[rows, :] = (edge_ref[rows, :].astype(F32) + message).astype(BF16)
        cot = cot_edge_ref[rows, :].astype(F32)
        upstream = live * (cot + dot_tn(pick_recv[:, rows], cot_fine_ref[...]))
        d_outer = (
            (upstream - row_mean(upstream) - normed * row_mean(upstream * normed)) * inv_scale
        ).astype(BF16)
        d_outer_all[rows, :] = d_outer
        d_hidden = dot_nt(d_outer, second_full)
        d_pre = (d_hidden * gate_sig * (1.0 + pre_act * (1.0 - gate_sig))).astype(BF16)
        d_pre_all[rows, :] = d_pre
        grad_edges_ref[rows, :] = (cot + dot_nt(d_pre, first_full[:width])).astype(BF16)
        d_send_all[rows, :] = dot_nt(d_pre, first_full[width : 2 * width]).astype(BF16)
        d_recv_all[rows, :] = dot_nt(d_pre, first_full[2 * width :]).astype(BF16)

    halo_back[...] = dot(
        pick_send[node_count : node_count + halo_count, :], d_send_all[...]
    ).astype(BF16)
    back = exchange(halo_back, returned, 0, back_sems)
    coarse_part = dot(pick_send[node_count + halo_count :, :], d_send_all[...]).astype(BF16)
    second_part = dot_tn(hidden[...], d_outer_all[...]).astype(BF16)
    spare = part_rows - weight_rows - coarse_rows
    for at in range(patches):
        own_coarse = coarse_part[at * coarse_rows : (at + 1) * coarse_rows]
        if spare:
            own_coarse = jnp.concatenate([own_coarse, jnp.zeros((spare, width), BF16)], axis=0)
        parts[at, first_rows:weight_rows, :] = second_part[at * second_rows : (at + 1) * second_rows]
        parts[at, weight_rows:, :] = own_coarse
    to_core = []
    held = PART_ROWS // first_rows
    for at in range(patches // held):
        part = dot_tn(
            joined[:, at * PART_ROWS : (at + 1) * PART_ROWS], d_pre_all[...]
        ).astype(BF16)
        for place in range(held):
            parts[at * held + place, :first_rows, :] = part[
                place * first_rows : (place + 1) * first_rows
            ]
        for chip in range(at * held // 2, (at + 1) * held // 2):
            to_core.append(
                send(
                    parts.at[2 * chip + 1 - c], from_core.at[chip], core_sems, (chip,), sibling
                )
            )

    to_grp = []
    for chip in range(chips):
        to_core[chip].wait_recv()
        chip_sum[chip] = (parts[2 * chip + c].astype(F32) + from_core[chip].astype(F32)).astype(
            BF16
        )
        to_grp.append(
            [
                send(
                    chip_sum.at[chip, :, columns((k + offset) % blocks)],
                    from_grp.at[offset - 1, chip],
                    grp_sems,
                    (chip, offset - 1),
                    peer(offset),
                )
                for offset in range(1, blocks)
            ]
        )
    fine_msg_ref[...] = dot(pick_recv[...], message_all[...]).astype(BF16)
    local_grad = dot(pick_send[:node_count, :], d_send_all[...]) + dot(
        pick_recv[...], d_recv_all[...]
    )
    for copy in back:
        copy.wait_recv()
    grad_fine_ref[...] = (
        local_grad + dot(picks(node_count, list_idx_ref[...]), returned[...])
    ).astype(BF16)
    for chip in range(chips):
        total = chip_sum[chip, :, columns(k)].astype(F32)
        for offset in range(1, blocks):
            to_grp[chip][offset - 1].wait_recv()
            total = total + from_grp[offset - 1, chip].astype(F32)
        plane_sum[chip] = total.astype(BF16)
    to_z = [
        send(
            plane_sum.at[chip_at(step)],
            from_z.at[step - 1],
            z_sems,
            (step - 1,),
            (a, 2 * chip_at(step) + c),
        )
        for step in range(1, chips)
    ]
    total = plane_sum[z].astype(F32)
    for step in range(1, chips):
        to_z[step - 1].wait_recv()
        total = total + from_z[step - 1].astype(F32)
    whole_sum[...] = total.astype(BF16)
    if far_count > 1:
        to_far = [
            send(
                whole_sum,
                from_far.at[step - 1],
                far_sems,
                (step - 1,),
                ((a + step * blocks) % groups, b),
            )
            for step in range(1, far_count)
        ]
        for step in range(1, far_count):
            to_far[step - 1].wait_recv()
            total = total + from_far[step - 1].astype(F32)
    result[:, columns(k)] = total.astype(BF16)
    shares = [
        send(
            result.at[:, columns(k)],
            result.at[:, columns(k)],
            result_sems,
            (offset - 1,),
            peer(offset),
        )
        for offset in range(1, blocks)
    ]
    for copy in shares:
        copy.wait_recv()
    grad_first_ref[...] = result[:first_rows, :].astype(F32)
    grad_second_ref[...] = result[first_rows:weight_rows, :].astype(F32)
    grad_coarse_ref[...] = result[weight_rows:, :].astype(F32)[:coarse_rows]
    for copy in pending:
        copy.wait_send()


def on_device(
    groups,
    patches,
    fine_latent,
    edge_latent,
    coarse_latent,
    first_proj,
    second_proj,
    senders,
    receivers,
    block_counts,
    send_rows,
    cot_edges,
    cot_fine,
):
    node_count, width = fine_latent.shape
    edge_count = edge_latent.shape[0]
    halo_count = send_rows.size
    table_rows = node_count + halo_count + coarse_latent.shape[0]
    first_rows = first_proj.shape[0]
    second_rows = second_proj.shape[0]
    coarse_rows = coarse_latent.shape[0] // patches
    weight_rows = first_rows + second_rows
    part_rows = weight_rows + -(-coarse_rows // ROW_TILE) * ROW_TILE
    chips = patches // 2
    blocks = width // LANES
    far = max(groups // blocks - 1, 1)
    vmem = pl.BlockSpec(memory_space=pltpu.VMEM)

    def sems(*shape):
        return pltpu.SemaphoreType.DMA((2,) + shape)

    return pl.pallas_call(
        functools.partial(kernel, groups, patches),
        out_shape=(
            jax.ShapeDtypeStruct((edge_count, width), BF16),
            jax.ShapeDtypeStruct((node_count, width), BF16),
            jax.ShapeDtypeStruct((edge_count, width), BF16),
            jax.ShapeDtypeStruct((node_count, width), BF16),
            jax.ShapeDtypeStruct((coarse_rows, width), F32),
            jax.ShapeDtypeStruct((first_rows, width), F32),
            jax.ShapeDtypeStruct((second_rows, width), F32),
        ),
        in_specs=[pl.BlockSpec(memory_space=pltpu.SMEM)] + [vmem] * 10,
        out_specs=(vmem,) * 7,
        scratch_shapes=[
            pltpu.VMEM((patches, weight_rows, width), BF16),
            pltpu.VMEM((halo_count, width), BF16),
            pltpu.VMEM((table_rows, width), BF16),
            pltpu.VMEM((table_rows, edge_count), BF16),
            pltpu.VMEM((node_count, edge_count), BF16),
            pltpu.VMEM((edge_count, 3 * width), BF16),
        ]
        + [pltpu.VMEM((edge_count, width), BF16)] * 6
        + [
            pltpu.VMEM((halo_count, width), BF16),
            pltpu.VMEM((halo_count, width), BF16),
            pltpu.VMEM((patches, part_rows, width), BF16),
            pltpu.VMEM((chips, part_rows, width), BF16),
            pltpu.VMEM((chips, part_rows, width), BF16),
            pltpu.VMEM((blocks - 1, chips, part_rows, LANES), BF16),
            pltpu.VMEM((chips, part_rows, LANES), BF16),
            pltpu.VMEM((chips - 1, part_rows, LANES), BF16),
            pltpu.VMEM((part_rows, LANES), BF16),
            pltpu.VMEM((far, part_rows, LANES), BF16),
            pltpu.VMEM((part_rows, width), BF16),
            sems(chips - 1),
            sems(chips - 1, blocks - 1),
            sems(chips),
            sems(4),
            sems(4),
            sems(chips),
            sems(chips, blocks - 1),
            sems(chips - 1),
            sems(far),
            sems(blocks - 1),
        ],
        compiler_params=pltpu.CompilerParams(
            collective_id=0, has_side_effects=True, vmem_limit_bytes=48 * 1024 * 1024
        ),
    )(
        block_counts,
        fine_latent,
        edge_latent,
        coarse_latent,
        first_proj,
        second_proj,
        senders.reshape(1, edge_count),
        receivers.reshape(1, edge_count),
        send_rows.reshape(1, halo_count),
        cot_edges,
        cot_fine,
    )


def solution(mesh):
    both = P(("grp", "patch"), None)
    flat = P(("grp", "patch"))
    rows = P("patch", None)
    return jax.shard_map(
        functools.partial(on_device, mesh.shape["grp"], mesh.shape["patch"]),
        mesh=mesh,
        in_specs=(both, both, P(), rows, rows, flat, flat, flat, both, both, both),
        out_specs=(both, both, both, both, rows, rows, rows),
        check_vma=False,
    )
```

```python
import functools

import jax
import jax.numpy as jnp
from jax import lax
from jax.experimental import pallas as pl
from jax.experimental.pallas import tpu as pltpu
from jax.sharding import PartitionSpec as P

norm_eps = 1e-05
LANES = 128
ROW_TILE = 16
EDGE_BLOCK = 256
PART_ROWS = 384
F32 = jnp.float32
BF16 = jnp.bfloat16


def dot(x, y):
    return jnp.dot(x, y, preferred_element_type=F32)


def dot_nt(x, y):
    return lax.dot_general(x, y, (((1,), (1,)), ((), ())), preferred_element_type=F32)


def dot_tn(x, y):
    return lax.dot_general(x, y, (((0,), (0,)), ((), ())), preferred_element_type=F32)


def picks(rows, index_row):
    where = lax.broadcasted_iota(jnp.int32, (rows, index_row.shape[1]), 0)
    return (where == index_row).astype(F32).astype(BF16)


def row_mean(x):
    return jnp.mean(x, axis=1, keepdims=True)


def kernel(
    groups,
    patches,
    counts_hbm,
    fine_hbm,
    edge_hbm,
    coarse_hbm,
    first_hbm,
    second_hbm,
    send_idx_hbm,
    recv_idx_hbm,
    list_idx_hbm,
    cot_edge_hbm,
    cot_fine_hbm,
    new_edges_hbm,
    fine_msg_hbm,
    grad_edges_hbm,
    grad_fine_hbm,
    result,
    counts_ref,
    send_idx_ref,
    recv_idx_ref,
    list_idx_ref,
    cot_edge_ref,
    cot_fine_ref,
    new_edges_ref,
    fine_msg_ref,
    grad_edges_ref,
    grad_fine_ref,
    weights,
    outgoing,
    table,
    pick_send,
    pick_recv,
    joined,
    hidden,
    d_outer_all,
    d_pre_all,
    message_all,
    d_send_all,
    d_recv_all,
    halo_back,
    returned,
    parts,
    from_core,
    chip_sum,
    from_grp,
    plane_sum,
    from_z,
    whole_sum,
    from_far,
    in_sems,
    out_sems,
    w_z_sems,
    w_grp_sems,
    w_core_sems,
    halo_sems,
    back_sems,
    core_sems,
    grp_sems,
    z_sems,
    far_sems,
    result_sems,
):
    a = lax.axis_index("grp")
    b = lax.axis_index("patch")
    z = b // 2
    c = b % 2
    chips = patches // 2
    width = fine_hbm.shape[1]
    blocks = width // LANES
    k = a % blocks
    base = a - k
    far_count = groups // blocks
    first_rows = first_hbm.shape[0]
    second_rows = second_hbm.shape[0]
    coarse_rows = coarse_hbm.shape[0] // patches
    node_count = fine_hbm.shape[0]
    list_rows = list_idx_hbm.shape[1]
    halo_count = 4 * list_rows
    edge_count = edge_hbm.shape[0]
    weight_rows = first_rows + second_rows
    part_rows = parts.shape[1]
    sibling = (a, 2 * z + 1 - c)
    pending = []

    def send(src, dst, sems, at, device):
        copy = pltpu.make_async_remote_copy(
            src_ref=src,
            dst_ref=dst,
            send_sem=sems.at[(0,) + at],
            recv_sem=sems.at[(1,) + at],
            device_id=device,
            device_id_type=pl.DeviceIdType.MESH,
        )
        copy.start()
        pending.append(copy)
        return copy

    def columns(block):
        return pl.ds(pl.multiple_of(block * LANES, LANES), LANES)

    def chip_at(offset):
        return (z + offset + chips) % chips

    def peer(offset):
        return (base + (k + offset) % blocks, b)

    def exchange(src, dst, first_row, sems):
        routes = (
            (1, 0, (a, (b + 1) % patches)),
            (0, 1, (a, (b + patches - 1) % patches)),
            (3, 2, ((a + 1) % groups, b)),
            (2, 3, ((a + groups - 1) % groups, b)),
        )
        return [
            send(
                src.at[pl.ds(own * list_rows, list_rows), :],
                dst.at[pl.ds(first_row + slot * list_rows, list_rows), :],
                sems,
                (slot,),
                device,
            )
            for own, slot, device in routes
        ]

    barrier = pltpu.get_barrier_semaphore()
    for step in range(1, patches):
        pl.semaphore_signal(
            barrier, inc=1, device_id=(a, (b + step) % patches), device_id_type=pl.DeviceIdType.MESH
        )
    for step in range(1, groups):
        pl.semaphore_signal(
            barrier, inc=1, device_id=((a + step) % groups, b), device_id_type=pl.DeviceIdType.MESH
        )
    fine_ref = table.at[:node_count, :]
    incoming = [
        pltpu.make_async_copy(src, dst, in_sems.at[at])
        for at, (src, dst) in enumerate(
            (
                (first_hbm, weights.at[b, :first_rows, :]),
                (second_hbm, weights.at[b, first_rows:, :]),
                (list_idx_hbm, list_idx_ref),
                (fine_hbm, fine_ref),
                (recv_idx_hbm, recv_idx_ref),
                (send_idx_hbm, send_idx_ref),
                (edge_hbm, joined.at[:, :width]),
                (coarse_hbm, table.at[node_count + halo_count :, :]),
                (counts_hbm, counts_ref),
                (cot_edge_hbm, cot_edge_ref),
                (cot_fine_hbm, cot_fine_ref),
            )
        )
    ]
    for copy in incoming:
        copy.start()
    for copy in incoming[2:4]:
        copy.wait()
    for own in range(4):
        outgoing[own * list_rows : (own + 1) * list_rows, :] = dot_tn(
            picks(node_count, list_idx_ref[own : own + 1, :]), fine_ref[...]
        ).astype(BF16)
    for copy in incoming[:2]:
        copy.wait()
    pl.semaphore_wait(barrier, patches + groups - 2)

    along_z = [
        send(
            weights.at[b, :, columns(k)],
            weights.at[b, :, columns(k)],
            w_z_sems,
            (step - 1,),
            (a, 2 * chip_at(step) + c),
        )
        for step in range(1, chips)
    ]
    between = [send(weights.at[b], weights.at[b], w_core_sems, (0,), sibling)]
    halo = exchange(outgoing, table, node_count, halo_sems)
    for copy in incoming[4:]:
        copy.wait()
    over_grp = []
    for step in range(1, chips):
        along_z[step - 1].wait_recv()
        owner = 2 * chip_at(-step) + c
        over_grp.append(
            [
                send(
                    weights.at[owner, :, columns(k)],
                    weights.at[owner, :, columns(k)],
                    w_grp_sems,
                    (step - 1, offset - 1),
                    peer(offset),
                )
                for offset in range(1, blocks)
            ]
        )
    pick_send[...] = picks(table.shape[0], send_idx_ref[...])
    pick_recv[...] = picks(node_count, recv_idx_ref[...])
    joined[:, 2 * width :] = dot_tn(pick_recv[...], fine_ref[...]).astype(BF16)
    for step in range(1, chips):
        for copy in over_grp[step - 1]:
            copy.wait_recv()
        owner = 2 * chip_at(-step) + c
        between.append(
            send(weights.at[owner], weights.at[owner], w_core_sems, (step,), sibling)
        )
    for copy in halo:
        copy.wait_recv()
    joined[:, width : 2 * width] = dot_tn(pick_send[...], table[...]).astype(BF16)
    for copy in between:
        copy.wait_recv()

    @pl.loop(0, edge_count // EDGE_BLOCK)
    def _(at):
        rows = pl.ds(pl.multiple_of(at * EDGE_BLOCK, EDGE_BLOCK), EDGE_BLOCK)
        first_full = weights[:, :first_rows, :].reshape(patches * first_rows, width)
        second_full = weights[:, first_rows:, :].reshape(patches * second_rows, width)
        pre_act = dot(joined[rows, :], first_full)
        gate_sig = 1.0 / (1.0 + jnp.exp(-pre_act))
        hid = (pre_act * gate_sig).astype(BF16)
        hidden[rows, :] = hid
        outer_proj = dot(hid, second_full)
        centre = outer_proj - row_mean(outer_proj)
        inv_scale = 1.0 / jnp.sqrt(row_mean(centre * centre) + norm_eps)
        normed = centre * inv_scale
        position = lax.broadcasted_iota(jnp.int32, (EDGE_BLOCK, 1), 0)
        per = EDGE_BLOCK // LANES
        bound = counts_ref[at * per]
        for extra in range(1, per):
            bound = jnp.where(
                position < extra * LANES, bound, counts_ref[at * per + extra] + extra * LANES
            )
        live = (position < bound).astype(F32)
        message = live * normed
        message_all[rows, :] = message.astype(BF16)
        new_edges_ref[rows, :] = (joined[rows, :width].astype(F32) + message).astype(BF16)
        cot = cot_edge_ref[rows, :].astype(F32)
        upstream = live * (cot + dot_tn(pick_recv[:, rows], cot_fine_ref[...]))
        d_outer = (
            (upstream - row_mean(upstream) - normed * row_mean(upstream * normed)) * inv_scale
        ).astype(BF16)
        d_outer_all[rows, :] = d_outer
        d_hidden = dot_nt(d_outer, second_full)
        d_pre = (d_hidden * gate_sig * (1.0 + pre_act * (1.0 - gate_sig))).astype(BF16)
        d_pre_all[rows, :] = d_pre
        grad_edges_ref[rows, :] = (cot + dot_nt(d_pre, first_full[:width])).astype(BF16)
        d_send_all[rows, :] = dot_nt(d_pre, first_full[width : 2 * width]).astype(BF16)
        d_recv_all[rows, :] = dot_nt(d_pre, first_full[2 * width :]).astype(BF16)

    leaving = [
        pltpu.make_async_copy(new_edges_ref, new_edges_hbm, out_sems.at[0]),
        pltpu.make_async_copy(grad_edges_ref, grad_edges_hbm, out_sems.at[1]),
    ]
    for copy in leaving:
        copy.start()

    halo_back[...] = dot(
        pick_send[node_count : node_count + halo_count, :], d_send_all[...]
    ).astype(BF16)
    back = exchange(halo_back, returned, 0, back_sems)
    coarse_part = dot(pick_send[node_count + halo_count :, :], d_send_all[...]).astype(BF16)
    second_part = dot_tn(hidden[...], d_outer_all[...]).astype(BF16)
    spare = part_rows - weight_rows - coarse_rows
    for at in range(patches):
        own_coarse = coarse_part[at * coarse_rows : (at + 1) * coarse_rows]
        if spare:
            own_coarse = jnp.concatenate([own_coarse, jnp.zeros((spare, width), BF16)], axis=0)
        parts[at, first_rows:weight_rows, :] = second_part[at * second_rows : (at + 1) * second_rows]
        parts[at, weight_rows:, :] = own_coarse
    to_core = []
    held = PART_ROWS // first_rows
    for at in range(patches // held):
        part = dot_tn(
            joined[:, at * PART_ROWS : (at + 1) * PART_ROWS], d_pre_all[...]
        ).astype(BF16)
        for place in range(held):
            parts[at * held + place, :first_rows, :] = part[
                place * first_rows : (place + 1) * first_rows
            ]
    for turn in range(chips):
        chip = chip_at(turn)
        to_core.append(
            send(parts.at[2 * chip + 1 - c], from_core.at[chip], core_sems, (turn,), sibling)
        )

    turns = list(range(1, chips)) + [0]
    to_grp = []
    for turn in turns:
        chip = chip_at(turn)
        to_core[turn].wait_recv()
        chip_sum[chip] = (parts[2 * chip + c].astype(F32) + from_core[chip].astype(F32)).astype(
            BF16
        )
        to_grp.append(
            [
                send(
                    chip_sum.at[chip, :, columns((k + offset) % blocks)],
                    from_grp.at[offset - 1, turn],
                    grp_sems,
                    (turn, offset - 1),
                    peer(offset),
                )
                for offset in range(1, blocks)
            ]
        )
    to_z = []
    for turn in turns:
        chip = chip_at(turn)
        total = chip_sum[chip, :, columns(k)].astype(F32)
        for offset in range(1, blocks):
            to_grp[turn - 1][offset - 1].wait_recv()
            total = total + from_grp[offset - 1, turn].astype(F32)
        if turn:
            plane_sum[turn - 1] = total.astype(BF16)
            to_z.append(
                send(
                    plane_sum.at[turn - 1],
                    from_z.at[turn - 1],
                    z_sems,
                    (turn - 1,),
                    (a, 2 * chip + c),
                )
            )
    fine_msg_ref[...] = dot(pick_recv[...], message_all[...]).astype(BF16)
    local_grad = dot(pick_send[:node_count, :], d_send_all[...]) + dot(
        pick_recv[...], d_recv_all[...]
    )
    for own in range(4):
        back[own].wait_recv()
    for own in range(4):
        local_grad = local_grad + dot(
            picks(node_count, list_idx_ref[own : own + 1, :]),
            returned[own * list_rows : (own + 1) * list_rows, :],
        )
    grad_fine_ref[...] = local_grad.astype(BF16)
    leaving += [
        pltpu.make_async_copy(fine_msg_ref, fine_msg_hbm, out_sems.at[2]),
        pltpu.make_async_copy(grad_fine_ref, grad_fine_hbm, out_sems.at[3]),
    ]
    for copy in leaving[2:]:
        copy.start()
    for step in range(1, chips):
        to_z[step - 1].wait_recv()
        total = total + from_z[step - 1].astype(F32)
    whole_sum[...] = total.astype(BF16)
    if far_count > 1:
        to_far = [
            send(
                whole_sum,
                from_far.at[step - 1],
                far_sems,
                (step - 1,),
                ((a + step * blocks) % groups, b),
            )
            for step in range(1, far_count)
        ]
        for step in range(1, far_count):
            to_far[step - 1].wait_recv()
            total = total + from_far[step - 1].astype(F32)
    result[:, columns(k)] = total.astype(BF16)
    shares = [
        send(
            result.at[:, columns(k)],
            result.at[:, columns(k)],
            result_sems,
            (offset - 1,),
            peer(offset),
        )
        for offset in range(1, blocks)
    ]
    for copy in shares:
        copy.wait_recv()
    for copy in leaving:
        copy.wait()
    for copy in pending:
        copy.wait_send()


def finish(first_rows, second_rows, result, *refs):
    sources, targets, shares, sems = refs[:4], refs[4:8], refs[8:11], refs[11]
    copies = [
        pltpu.make_async_copy(source, target, sems.at[at])
        for at, (source, target) in enumerate(zip(sources, targets))
    ]
    for copy in copies:
        copy.start()
    weight_rows = first_rows + second_rows
    shares[0][...] = result[weight_rows:, :].astype(F32)[: shares[0].shape[0]]
    shares[1][...] = result[:first_rows, :].astype(F32)
    shares[2][...] = result[first_rows:weight_rows, :].astype(F32)
    for copy in copies:
        copy.wait()


def on_device(
    groups,
    patches,
    fine_latent,
    edge_latent,
    coarse_latent,
    first_proj,
    second_proj,
    senders,
    receivers,
    block_counts,
    send_rows,
    cot_edges,
    cot_fine,
):
    node_count, width = fine_latent.shape
    edge_count = edge_latent.shape[0]
    halo_count = send_rows.size
    table_rows = node_count + halo_count + coarse_latent.shape[0]
    first_rows = first_proj.shape[0]
    second_rows = second_proj.shape[0]
    coarse_rows = coarse_latent.shape[0] // patches
    weight_rows = first_rows + second_rows
    part_rows = weight_rows + -(-coarse_rows // ROW_TILE) * ROW_TILE
    chips = patches // 2
    blocks = width // LANES
    far = max(groups // blocks - 1, 1)
    vmem = pl.BlockSpec(memory_space=pltpu.VMEM)
    hbm = pl.BlockSpec(memory_space=pltpu.HBM)

    def sems(*shape):
        return pltpu.SemaphoreType.DMA((2,) + shape)

    rows_out = (
        jax.ShapeDtypeStruct((edge_count, width), BF16),
        jax.ShapeDtypeStruct((node_count, width), BF16),
        jax.ShapeDtypeStruct((edge_count, width), BF16),
        jax.ShapeDtypeStruct((node_count, width), BF16),
    )
    *rows, result = pl.pallas_call(
        functools.partial(kernel, groups, patches),
        out_shape=rows_out + (jax.ShapeDtypeStruct((part_rows, width), BF16),),
        in_specs=[hbm] * 11,
        out_specs=(hbm,) * 4 + (vmem,),
        scratch_shapes=[
            pltpu.SMEM(block_counts.shape, jnp.int32),
            pltpu.VMEM((1, edge_count), jnp.int32),
            pltpu.VMEM((1, edge_count), jnp.int32),
            pltpu.VMEM(send_rows.shape, jnp.int32),
            pltpu.VMEM((edge_count, width), BF16),
            pltpu.VMEM((node_count, width), BF16),
            pltpu.VMEM((edge_count, width), BF16),
            pltpu.VMEM((node_count, width), BF16),
            pltpu.VMEM((edge_count, width), BF16),
            pltpu.VMEM((node_count, width), BF16),
            pltpu.VMEM((patches, weight_rows, width), BF16),
            pltpu.VMEM((halo_count, width), BF16),
            pltpu.VMEM((table_rows, width), BF16),
            pltpu.VMEM((table_rows, edge_count), BF16),
            pltpu.VMEM((node_count, edge_count), BF16),
            pltpu.VMEM((edge_count, 3 * width), BF16),
        ]
        + [pltpu.VMEM((edge_count, width), BF16)] * 6
        + [
            pltpu.VMEM((halo_count, width), BF16),
            pltpu.VMEM((halo_count, width), BF16),
            pltpu.VMEM((patches, part_rows, width), BF16),
            pltpu.VMEM((chips, part_rows, width), BF16),
            pltpu.VMEM((chips, part_rows, width), BF16),
            pltpu.VMEM((blocks - 1, chips, part_rows, LANES), BF16),
            pltpu.VMEM((chips - 1, part_rows, LANES), BF16),
            pltpu.VMEM((chips - 1, part_rows, LANES), BF16),
            pltpu.VMEM((part_rows, LANES), BF16),
            pltpu.VMEM((far, part_rows, LANES), BF16),
            pltpu.SemaphoreType.DMA((11,)),
            pltpu.SemaphoreType.DMA((4,)),
            sems(chips - 1),
            sems(chips - 1, blocks - 1),
            sems(chips),
            sems(4),
            sems(4),
            sems(chips),
            sems(chips, blocks - 1),
            sems(chips - 1),
            sems(far),
            sems(blocks - 1),
        ],
        compiler_params=pltpu.CompilerParams(
            collective_id=0, has_side_effects=True, vmem_limit_bytes=62 * 1024 * 1024
        ),
    )(
        block_counts,
        fine_latent,
        edge_latent,
        coarse_latent,
        first_proj,
        second_proj,
        senders.reshape(1, edge_count),
        receivers.reshape(1, edge_count),
        send_rows,
        cot_edges,
        cot_fine,
    )
    shares = tuple(
        jax.ShapeDtypeStruct((count, width), F32)
        for count in (coarse_rows, first_rows, second_rows)
    )
    return pl.pallas_call(
        functools.partial(finish, first_rows, second_rows),
        out_shape=rows_out + shares,
        in_specs=[vmem] * 5,
        out_specs=(hbm,) * 4 + (vmem,) * 3,
        scratch_shapes=[pltpu.SemaphoreType.DMA((4,))],
    )(result, *rows)


def solution(mesh):
    both = P(("grp", "patch"), None)
    flat = P(("grp", "patch"))
    rows = P("patch", None)
    return jax.shard_map(
        functools.partial(on_device, mesh.shape["grp"], mesh.shape["patch"]),
        mesh=mesh,
        in_specs=(both, both, P(), rows, rows, flat, flat, flat, both, both, both),
        out_specs=(both, both, both, both, rows, rows, rows),
        check_vma=False,
    )
```

```python
import functools

import jax
import jax.numpy as jnp
from jax import lax
from jax.experimental import pallas as pl
from jax.experimental.pallas import tpu as pltpu
from jax.sharding import PartitionSpec as P

norm_eps = 1e-05
LANES = 128
ROW_TILE = 16
EDGE_BLOCK = 256
PART_ROWS = 384
F32 = jnp.float32
BF16 = jnp.bfloat16


def dot(x, y):
    return jnp.dot(x, y, preferred_element_type=F32)


def dot_nt(x, y):
    return lax.dot_general(x, y, (((1,), (1,)), ((), ())), preferred_element_type=F32)


def dot_tn(x, y):
    return lax.dot_general(x, y, (((0,), (0,)), ((), ())), preferred_element_type=F32)


def picks(rows, index_row):
    where = lax.broadcasted_iota(jnp.int32, (rows, index_row.shape[1]), 0)
    return (where == index_row).astype(F32).astype(BF16)


def row_mean(x):
    return jnp.mean(x, axis=1, keepdims=True)


def kernel(
    groups,
    patches,
    counts_hbm,
    fine_hbm,
    edge_hbm,
    coarse_hbm,
    first_hbm,
    second_hbm,
    send_idx_hbm,
    recv_idx_hbm,
    list_idx_hbm,
    cot_edge_hbm,
    cot_fine_hbm,
    new_edges_hbm,
    fine_msg_hbm,
    grad_edges_hbm,
    grad_fine_hbm,
    result,
    counts_ref,
    send_idx_ref,
    recv_idx_ref,
    list_idx_ref,
    cot_edge_ref,
    cot_fine_ref,
    new_edges_ref,
    fine_msg_ref,
    grad_edges_ref,
    grad_fine_ref,
    weights,
    outgoing,
    table,
    pick_send,
    pick_recv,
    joined,
    hidden,
    d_outer_all,
    d_pre_all,
    message_all,
    upstream_all,
    d_send_all,
    d_recv_all,
    halo_back,
    returned,
    parts,
    from_core,
    chip_sum,
    from_one,
    pair_sum,
    from_two,
    plane_sum,
    from_z,
    whole_sum,
    from_far,
    in_sems,
    out_sems,
    w_z_sems,
    w_grp_sems,
    w_core_sems,
    halo_sems,
    back_sems,
    core_sems,
    grp_sems,
    z_sems,
    far_sems,
    result_sems,
):
    a = lax.axis_index("grp")
    b = lax.axis_index("patch")
    z = b // 2
    c = b % 2
    chips = patches // 2
    width = fine_hbm.shape[1]
    blocks = width // LANES
    k = a % blocks
    base = a - k
    far_count = groups // blocks
    first_rows = first_hbm.shape[0]
    second_rows = second_hbm.shape[0]
    coarse_rows = coarse_hbm.shape[0] // patches
    node_count = fine_hbm.shape[0]
    list_rows = list_idx_hbm.shape[1]
    halo_count = 4 * list_rows
    edge_count = edge_hbm.shape[0]
    weight_rows = first_rows + second_rows
    part_rows = parts.shape[1]
    sibling = (a, 2 * z + 1 - c)
    pending = []

    def send(src, dst, sems, at, device):
        copy = pltpu.make_async_remote_copy(
            src_ref=src,
            dst_ref=dst,
            send_sem=sems.at[(0,) + at],
            recv_sem=sems.at[(1,) + at],
            device_id=device,
            device_id_type=pl.DeviceIdType.MESH,
        )
        copy.start()
        pending.append(copy)
        return copy

    def columns(block):
        return pl.ds(pl.multiple_of(block * LANES, LANES), LANES)

    def chip_at(offset):
        return (z + offset + chips) % chips

    def peer(offset):
        return (base + (k + offset) % blocks, b)

    def exchange(src, dst, first_row, sems):
        routes = (
            (1, 0, (a, (b + 1) % patches)),
            (0, 1, (a, (b + patches - 1) % patches)),
            (3, 2, ((a + 1) % groups, b)),
            (2, 3, ((a + groups - 1) % groups, b)),
        )
        return [
            send(
                src.at[pl.ds(own * list_rows, list_rows), :],
                dst.at[pl.ds(first_row + slot * list_rows, list_rows), :],
                sems,
                (slot,),
                device,
            )
            for own, slot, device in routes
        ]

    barrier = pltpu.get_barrier_semaphore()
    for step in range(1, patches):
        pl.semaphore_signal(
            barrier, inc=1, device_id=(a, (b + step) % patches), device_id_type=pl.DeviceIdType.MESH
        )
    for step in range(1, groups):
        pl.semaphore_signal(
            barrier, inc=1, device_id=((a + step) % groups, b), device_id_type=pl.DeviceIdType.MESH
        )
    fine_ref = table.at[:node_count, :]
    incoming = [
        pltpu.make_async_copy(src, dst, in_sems.at[at])
        for at, (src, dst) in enumerate(
            (
                (first_hbm, weights.at[b, :first_rows, :]),
                (second_hbm, weights.at[b, first_rows:, :]),
                (list_idx_hbm, list_idx_ref),
                (fine_hbm, fine_ref),
                (recv_idx_hbm, recv_idx_ref),
                (send_idx_hbm, send_idx_ref),
                (edge_hbm, joined.at[:, :width]),
                (coarse_hbm, table.at[node_count + halo_count :, :]),
                (counts_hbm, counts_ref),
                (cot_edge_hbm, cot_edge_ref),
                (cot_fine_hbm, cot_fine_ref),
            )
        )
    ]
    for copy in incoming:
        copy.start()
    for copy in incoming[:2]:
        copy.wait()
    pl.semaphore_wait(barrier, patches + groups - 2)

    order = [step for near in range(1, chips) for step in (near, chips - near)][: chips - 1]
    along_z = {}

    def start_z(step):
        along_z[step] = send(
            weights.at[b, :, columns(k)],
            weights.at[b, :, columns(k)],
            w_z_sems,
            (step - 1,),
            (a, 2 * chip_at(step) + c),
        )

    for step in order[:2]:
        start_z(step)
    between = [send(weights.at[b], weights.at[b], w_core_sems, (0,), sibling)]
    for copy in incoming[2:4]:
        copy.wait()
    for own in range(4):
        outgoing[own * list_rows : (own + 1) * list_rows, :] = dot_tn(
            picks(node_count, list_idx_ref[own : own + 1, :]), fine_ref[...]
        ).astype(BF16)
    halo = exchange(outgoing, table, node_count, halo_sems)
    for copy in incoming[4:]:
        copy.wait()
    over_grp = {}
    for at, step in enumerate(order):
        along_z[step].wait_recv()
        for later in order[at + 2 : at + 3]:
            start_z(later)
        owner = 2 * chip_at(-step) + c
        over_grp[step] = [
            send(
                weights.at[owner, :, columns(k)],
                weights.at[owner, :, columns(k)],
                w_grp_sems,
                (step - 1, offset - 1),
                peer(offset),
            )
            for offset in range(1, blocks)
        ]
    pick_send[...] = picks(table.shape[0], send_idx_ref[...])
    pick_recv[...] = picks(node_count, recv_idx_ref[...])
    joined[:, 2 * width :] = dot_tn(pick_recv[...], fine_ref[...]).astype(BF16)
    upstream_all[...] = cot_edge_ref[...].astype(F32) + dot_tn(pick_recv[...], cot_fine_ref[...])
    for step in order:
        for copy in over_grp[step]:
            copy.wait_recv()
        owner = 2 * chip_at(-step) + c
        between.append(
            send(weights.at[owner], weights.at[owner], w_core_sems, (step,), sibling)
        )
    for copy in halo:
        copy.wait_recv()
    joined[:, width : 2 * width] = dot_tn(pick_send[...], table[...]).astype(BF16)
    for copy in between:
        copy.wait_recv()

    @pl.loop(0, edge_count // EDGE_BLOCK)
    def _(at):
        rows = pl.ds(pl.multiple_of(at * EDGE_BLOCK, EDGE_BLOCK), EDGE_BLOCK)
        first_full = weights[:, :first_rows, :].reshape(patches * first_rows, width)
        second_full = weights[:, first_rows:, :].reshape(patches * second_rows, width)
        pre_act = dot(joined[rows, :], first_full)
        gate_sig = 1.0 / (1.0 + jnp.exp(-pre_act))
        hid = (pre_act * gate_sig).astype(BF16)
        hidden[rows, :] = hid
        outer_proj = dot(hid, second_full)
        centre = outer_proj - row_mean(outer_proj)
        inv_scale = 1.0 / jnp.sqrt(row_mean(centre * centre) + norm_eps)
        normed = centre * inv_scale
        position = lax.broadcasted_iota(jnp.int32, (EDGE_BLOCK, 1), 0)
        per = EDGE_BLOCK // LANES
        bound = counts_ref[at * per]
        for extra in range(1, per):
            bound = jnp.where(
                position < extra * LANES, bound, counts_ref[at * per + extra] + extra * LANES
            )
        live = (position < bound).astype(F32)
        message = live * normed
        message_all[rows, :] = message
        upstream = live * upstream_all[rows, :]
        d_outer = (
            (upstream - row_mean(upstream) - normed * row_mean(upstream * normed)) * inv_scale
        ).astype(BF16)
        d_outer_all[rows, :] = d_outer
        d_hidden = dot_nt(d_outer, second_full)
        d_pre = (d_hidden * gate_sig * (1.0 + pre_act * (1.0 - gate_sig))).astype(BF16)
        d_pre_all[rows, :] = d_pre
        d_send_all[rows, :] = dot_nt(d_pre, first_full[width : 2 * width]).astype(BF16)

    halo_back[...] = dot(
        pick_send[node_count : node_count + halo_count, :], d_send_all[...]
    ).astype(BF16)
    back = exchange(halo_back, returned, 0, back_sems)
    coarse_part = dot(pick_send[node_count + halo_count :, :], d_send_all[...]).astype(BF16)
    second_part = dot_tn(hidden[...], d_outer_all[...]).astype(BF16)
    spare = part_rows - weight_rows - coarse_rows
    for at in range(patches):
        own_coarse = coarse_part[at * coarse_rows : (at + 1) * coarse_rows]
        if spare:
            own_coarse = jnp.concatenate([own_coarse, jnp.zeros((spare, width), BF16)], axis=0)
        parts[at, first_rows:weight_rows, :] = second_part[at * second_rows : (at + 1) * second_rows]
        parts[at, weight_rows:, :] = own_coarse
    turns = list(range(1, chips)) + [0]
    k_hi, k_lo = k // 2, k % 2
    across_lo = (base + 2 * k_hi + 1 - k_lo, b)
    across_hi = (base + 2 * (1 - k_hi) + k_lo, b)
    to_core, to_one, to_two, to_z = {}, {}, {}, []
    pair_rows = 2 * first_rows
    by_chip = pair_rows % LANES == 0

    def form(turn):
        chip = chip_at(turn)
        if by_chip:
            span = pl.ds(pl.multiple_of(chip * pair_rows, LANES), pair_rows)
            part = dot_tn(joined[:, span], d_pre_all[...]).astype(BF16)
            parts[2 * chip, :first_rows, :] = part[:first_rows]
            parts[2 * chip + 1, :first_rows, :] = part[first_rows:]
        to_core[turn] = send(
            parts.at[2 * chip + 1 - c], from_core.at[turn], core_sems, (turn,), sibling
        )

    def sum_cores(turn):
        chip = chip_at(turn)
        to_core[turn].wait_recv()
        for hi in range(2):
            for lo in range(2):
                block = 2 * hi + lo
                span = slice(block * LANES, (block + 1) * LANES)
                chip_sum[turn, hi, lo] = (
                    parts[2 * chip + c, :, span].astype(F32) + from_core[turn, :, span].astype(F32)
                ).astype(BF16)
        if turn % 2:
            source, device = chip_sum.at[turn, :, 1 - k_lo], across_lo
        else:
            source, device = chip_sum.at[turn, 1 - k_hi], across_hi
        to_one[turn] = send(source, from_one.at[turn], grp_sems, (turn, 0), device)

    def sum_pair(turn):
        to_one[turn].wait_recv()
        for half in range(2):
            own = chip_sum[turn, half, k_lo] if turn % 2 else chip_sum[turn, k_hi, half]
            pair_sum[turn, half] = (own.astype(F32) + from_one[turn, half].astype(F32)).astype(
                BF16
            )
        other, device = (1 - k_hi, across_hi) if turn % 2 else (1 - k_lo, across_lo)
        to_two[turn] = send(
            pair_sum.at[turn, other], from_two.at[turn], grp_sems, (turn, 1), device
        )

    def sum_plane(turn):
        chip = chip_at(turn)
        to_two[turn].wait_recv()
        own = pair_sum[turn, k_hi if turn % 2 else k_lo]
        total = own.astype(F32) + from_two[turn].astype(F32)
        if turn:
            plane_sum[turn - 1] = total.astype(BF16)
            to_z.append(
                send(
                    plane_sum.at[turn - 1],
                    from_z.at[turn - 1],
                    z_sems,
                    (turn - 1,),
                    (a, 2 * chip + c),
                )
            )
        return total

    if not by_chip:
        held = PART_ROWS // first_rows
        for at in range(patches // held):
            part = dot_tn(
                joined[:, at * PART_ROWS : (at + 1) * PART_ROWS], d_pre_all[...]
            ).astype(BF16)
            for place in range(held):
                parts[at * held + place, :first_rows, :] = part[
                    place * first_rows : (place + 1) * first_rows
                ]
    def finish_edges():
        new_edges_ref[...] = (joined[:, :width].astype(F32) + message_all[...]).astype(BF16)
        first_full = weights[:, :first_rows, :].reshape(patches * first_rows, width)
        grad_edges_ref[...] = (
            cot_edge_ref[...].astype(F32) + dot_nt(d_pre_all[...], first_full[:width])
        ).astype(BF16)
        d_recv_all[...] = dot_nt(d_pre_all[...], first_full[2 * width :]).astype(BF16)
        leave(new_edges_ref, new_edges_hbm, 0)
        leave(grad_edges_ref, grad_edges_hbm, 1)

    def finish_nodes():
        fine_msg_ref[...] = dot(pick_recv[...], message_all[...].astype(BF16)).astype(BF16)
        local_grad = dot(pick_send[:node_count, :], d_send_all[...]) + dot(
            pick_recv[...], d_recv_all[...]
        )
        for own in range(4):
            back[own].wait_recv()
        for own in range(4):
            local_grad = local_grad + dot(
                picks(node_count, list_idx_ref[own : own + 1, :]),
                returned[own * list_rows : (own + 1) * list_rows, :],
            )
        grad_fine_ref[...] = local_grad.astype(BF16)
        leave(fine_msg_ref, fine_msg_hbm, 2)
        leave(grad_fine_ref, grad_fine_hbm, 3)

    leaving = []

    def leave(source, target, at):
        copy = pltpu.make_async_copy(source, target, out_sems.at[at])
        copy.start()
        leaving.append(copy)

    stages = (form, sum_cores, sum_pair, sum_plane)
    for at in range(chips + len(stages) - 1):
        for delay, stage in enumerate(stages):
            if 0 <= at - delay < chips:
                total = stage(turns[at - delay])
        if at == chips:
            finish_edges()
        if at == chips + 1:
            finish_nodes()
    for step in range(1, chips):
        to_z[step - 1].wait_recv()
        total = total + from_z[step - 1].astype(F32)
    whole_sum[...] = total.astype(BF16)
    if far_count > 1:
        to_far = [
            send(
                whole_sum,
                from_far.at[step - 1],
                far_sems,
                (step - 1,),
                ((a + step * blocks) % groups, b),
            )
            for step in range(1, far_count)
        ]
        for step in range(1, far_count):
            to_far[step - 1].wait_recv()
            total = total + from_far[step - 1].astype(F32)
    result[:, columns(k)] = total.astype(BF16)
    shares = [
        send(
            result.at[:, columns(k)],
            result.at[:, columns(k)],
            result_sems,
            (offset - 1,),
            peer(offset),
        )
        for offset in range(1, blocks)
    ]
    for copy in shares:
        copy.wait_recv()
    for copy in leaving:
        copy.wait()
    for copy in pending:
        copy.wait_send()


def finish(first_rows, second_rows, result, *refs):
    sources, targets, shares, sems = refs[:4], refs[4:8], refs[8:11], refs[11]
    copies = [
        pltpu.make_async_copy(source, target, sems.at[at])
        for at, (source, target) in enumerate(zip(sources, targets))
    ]
    for copy in copies:
        copy.start()
    weight_rows = first_rows + second_rows
    shares[0][...] = result[weight_rows:, :].astype(F32)[: shares[0].shape[0]]
    shares[1][...] = result[:first_rows, :].astype(F32)
    shares[2][...] = result[first_rows:weight_rows, :].astype(F32)
    for copy in copies:
        copy.wait()


def on_device(
    groups,
    patches,
    fine_latent,
    edge_latent,
    coarse_latent,
    first_proj,
    second_proj,
    senders,
    receivers,
    block_counts,
    send_rows,
    cot_edges,
    cot_fine,
):
    node_count, width = fine_latent.shape
    edge_count = edge_latent.shape[0]
    halo_count = send_rows.size
    table_rows = node_count + halo_count + coarse_latent.shape[0]
    first_rows = first_proj.shape[0]
    second_rows = second_proj.shape[0]
    coarse_rows = coarse_latent.shape[0] // patches
    weight_rows = first_rows + second_rows
    part_rows = weight_rows + -(-coarse_rows // ROW_TILE) * ROW_TILE
    chips = patches // 2
    blocks = width // LANES
    far = max(groups // blocks - 1, 1)
    vmem = pl.BlockSpec(memory_space=pltpu.VMEM)
    hbm = pl.BlockSpec(memory_space=pltpu.HBM)

    def sems(*shape):
        return pltpu.SemaphoreType.DMA((2,) + shape)

    rows_out = (
        jax.ShapeDtypeStruct((edge_count, width), BF16),
        jax.ShapeDtypeStruct((node_count, width), BF16),
        jax.ShapeDtypeStruct((edge_count, width), BF16),
        jax.ShapeDtypeStruct((node_count, width), BF16),
    )
    *rows, result = pl.pallas_call(
        functools.partial(kernel, groups, patches),
        out_shape=rows_out + (jax.ShapeDtypeStruct((part_rows, width), BF16),),
        in_specs=[hbm] * 11,
        out_specs=(hbm,) * 4 + (vmem,),
        scratch_shapes=[
            pltpu.SMEM(block_counts.shape, jnp.int32),
            pltpu.VMEM((1, edge_count), jnp.int32),
            pltpu.VMEM((1, edge_count), jnp.int32),
            pltpu.VMEM(send_rows.shape, jnp.int32),
            pltpu.VMEM((edge_count, width), BF16),
            pltpu.VMEM((node_count, width), BF16),
            pltpu.VMEM((edge_count, width), BF16),
            pltpu.VMEM((node_count, width), BF16),
            pltpu.VMEM((edge_count, width), BF16),
            pltpu.VMEM((node_count, width), BF16),
            pltpu.VMEM((patches, weight_rows, width), BF16),
            pltpu.VMEM((halo_count, width), BF16),
            pltpu.VMEM((table_rows, width), BF16),
            pltpu.VMEM((table_rows, edge_count), BF16),
            pltpu.VMEM((node_count, edge_count), BF16),
            pltpu.VMEM((edge_count, 3 * width), BF16),
        ]
        + [pltpu.VMEM((edge_count, width), BF16)] * 3
        + [pltpu.VMEM((edge_count, width), F32)] * 2
        + [pltpu.VMEM((edge_count, width), BF16)] * 2
        + [
            pltpu.VMEM((halo_count, width), BF16),
            pltpu.VMEM((halo_count, width), BF16),
            pltpu.VMEM((patches, part_rows, width), BF16),
            pltpu.VMEM((chips, part_rows, width), BF16),
            pltpu.VMEM((chips, 2, 2, part_rows, LANES), BF16),
            pltpu.VMEM((chips, 2, part_rows, LANES), BF16),
            pltpu.VMEM((chips, 2, part_rows, LANES), BF16),
            pltpu.VMEM((chips, part_rows, LANES), BF16),
            pltpu.VMEM((chips - 1, part_rows, LANES), BF16),
            pltpu.VMEM((chips - 1, part_rows, LANES), BF16),
            pltpu.VMEM((part_rows, LANES), BF16),
            pltpu.VMEM((far, part_rows, LANES), BF16),
            pltpu.SemaphoreType.DMA((11,)),
            pltpu.SemaphoreType.DMA((4,)),
            sems(chips - 1),
            sems(chips - 1, blocks - 1),
            sems(chips),
            sems(4),
            sems(4),
            sems(chips),
            sems(chips, 2),
            sems(chips - 1),
            sems(far),
            sems(blocks - 1),
        ],
        compiler_params=pltpu.CompilerParams(
            collective_id=0, has_side_effects=True, vmem_limit_bytes=62 * 1024 * 1024
        ),
    )(
        block_counts,
        fine_latent,
        edge_latent,
        coarse_latent,
        first_proj,
        second_proj,
        senders.reshape(1, edge_count),
        receivers.reshape(1, edge_count),
        send_rows,
        cot_edges,
        cot_fine,
    )
    shares = tuple(
        jax.ShapeDtypeStruct((count, width), F32)
        for count in (coarse_rows, first_rows, second_rows)
    )
    return pl.pallas_call(
        functools.partial(finish, first_rows, second_rows),
        out_shape=rows_out + shares,
        in_specs=[vmem] * 5,
        out_specs=(hbm,) * 4 + (vmem,) * 3,
        scratch_shapes=[pltpu.SemaphoreType.DMA((4,))],
    )(result, *rows)


def solution(mesh):
    both = P(("grp", "patch"), None)
    flat = P(("grp", "patch"))
    rows = P("patch", None)
    return jax.shard_map(
        functools.partial(on_device, mesh.shape["grp"], mesh.shape["patch"]),
        mesh=mesh,
        in_specs=(both, both, P(), rows, rows, flat, flat, flat, both, both, both),
        out_specs=(both, both, both, both, rows, rows, rows),
        check_vma=False,
    )
```

```python
import functools

import jax
import jax.numpy as jnp
from jax import lax
from jax.experimental import pallas as pl
from jax.experimental.pallas import tpu as pltpu
from jax.sharding import PartitionSpec as P

norm_eps = 1e-05
LANES = 128
ROW_TILE = 16
EDGE_BLOCK = 256
PART_ROWS = 384
F32 = jnp.float32
BF16 = jnp.bfloat16


def dot(x, y):
    return jnp.dot(x, y, preferred_element_type=F32)


def dot_nt(x, y):
    return lax.dot_general(x, y, (((1,), (1,)), ((), ())), preferred_element_type=F32)


def dot_tn(x, y):
    return lax.dot_general(x, y, (((0,), (0,)), ((), ())), preferred_element_type=F32)


def picks(rows, index_row):
    where = lax.broadcasted_iota(jnp.int32, (rows, index_row.shape[1]), 0)
    return (where == index_row).astype(F32).astype(BF16)


def row_mean(x):
    return jnp.mean(x, axis=1, keepdims=True)


def kernel(
    groups,
    patches,
    counts_hbm,
    fine_hbm,
    edge_hbm,
    coarse_hbm,
    first_hbm,
    second_hbm,
    send_idx_hbm,
    recv_idx_hbm,
    list_idx_hbm,
    cot_edge_hbm,
    cot_fine_hbm,
    new_edges_hbm,
    fine_msg_hbm,
    grad_edges_hbm,
    grad_fine_hbm,
    result,
    counts_ref,
    send_idx_ref,
    recv_idx_ref,
    list_idx_ref,
    cot_edge_ref,
    cot_fine_ref,
    new_edges_ref,
    fine_msg_ref,
    grad_edges_ref,
    grad_fine_ref,
    weights,
    outgoing,
    table,
    pick_send,
    pick_recv,
    joined,
    hidden,
    d_outer_all,
    d_pre_all,
    message_all,
    upstream_all,
    d_send_all,
    d_recv_all,
    halo_back,
    returned,
    parts,
    from_core,
    chip_sum,
    from_grp,
    plane_sum,
    from_z,
    whole_sum,
    from_far,
    in_sems,
    out_sems,
    w_z_sems,
    w_grp_sems,
    w_core_sems,
    halo_sems,
    back_sems,
    core_sems,
    grp_sems,
    z_sems,
    far_sems,
    result_sems,
):
    a = lax.axis_index("grp")
    b = lax.axis_index("patch")
    z = b // 2
    c = b % 2
    chips = patches // 2
    width = fine_hbm.shape[1]
    blocks = width // LANES
    k = a % blocks
    base = a - k
    far_count = groups // blocks
    first_rows = first_hbm.shape[0]
    second_rows = second_hbm.shape[0]
    coarse_rows = coarse_hbm.shape[0] // patches
    node_count = fine_hbm.shape[0]
    list_rows = list_idx_hbm.shape[1]
    halo_count = 4 * list_rows
    edge_count = edge_hbm.shape[0]
    weight_rows = first_rows + second_rows
    part_rows = parts.shape[1]
    sibling = (a, 2 * z + 1 - c)
    pending = []

    def send(src, dst, sems, at, device):
        copy = pltpu.make_async_remote_copy(
            src_ref=src,
            dst_ref=dst,
            send_sem=sems.at[(0,) + at],
            recv_sem=sems.at[(1,) + at],
            device_id=device,
            device_id_type=pl.DeviceIdType.MESH,
        )
        copy.start()
        pending.append(copy)
        return copy

    def columns(block):
        return pl.ds(pl.multiple_of(block * LANES, LANES), LANES)

    def chip_at(offset):
        return (z + offset + chips) % chips

    def peer(offset):
        return (base + (k + offset) % blocks, b)

    def exchange(src, dst, first_row, sems):
        routes = (
            (1, 0, (a, (b + 1) % patches)),
            (0, 1, (a, (b + patches - 1) % patches)),
            (3, 2, ((a + 1) % groups, b)),
            (2, 3, ((a + groups - 1) % groups, b)),
        )
        return [
            send(
                src.at[pl.ds(own * list_rows, list_rows), :],
                dst.at[pl.ds(first_row + slot * list_rows, list_rows), :],
                sems,
                (slot,),
                device,
            )
            for own, slot, device in routes
        ]

    barrier = pltpu.get_barrier_semaphore()
    for step in range(1, patches):
        pl.semaphore_signal(
            barrier, inc=1, device_id=(a, (b + step) % patches), device_id_type=pl.DeviceIdType.MESH
        )
    for step in range(1, groups):
        pl.semaphore_signal(
            barrier, inc=1, device_id=((a + step) % groups, b), device_id_type=pl.DeviceIdType.MESH
        )
    fine_ref = table.at[:node_count, :]
    incoming = [
        pltpu.make_async_copy(src, dst, in_sems.at[at])
        for at, (src, dst) in enumerate(
            (
                (first_hbm, weights.at[b, :first_rows, :]),
                (second_hbm, weights.at[b, first_rows:, :]),
                (list_idx_hbm, list_idx_ref),
                (fine_hbm, fine_ref),
                (recv_idx_hbm, recv_idx_ref),
                (send_idx_hbm, send_idx_ref),
                (edge_hbm, joined.at[:, :width]),
                (coarse_hbm, table.at[node_count + halo_count :, :]),
                (counts_hbm, counts_ref),
                (cot_edge_hbm, cot_edge_ref),
                (cot_fine_hbm, cot_fine_ref),
            )
        )
    ]
    for copy in incoming:
        copy.start()
    for copy in incoming[:2]:
        copy.wait()
    pl.semaphore_wait(barrier, patches + groups - 2)

    order = [step for near in range(1, chips) for step in (near, chips - near)][: chips - 1]
    along_z = {}

    def start_z(step):
        along_z[step] = send(
            weights.at[b, :, columns(k)],
            weights.at[b, :, columns(k)],
            w_z_sems,
            (step - 1,),
            (a, 2 * chip_at(step) + c),
        )

    for step in order[:2]:
        start_z(step)
    between = [send(weights.at[b], weights.at[b], w_core_sems, (0,), sibling)]
    for copy in incoming[2:4]:
        copy.wait()
    for own in range(4):
        outgoing[own * list_rows : (own + 1) * list_rows, :] = dot_tn(
            picks(node_count, list_idx_ref[own : own + 1, :]), fine_ref[...]
        ).astype(BF16)
    halo = exchange(outgoing, table, node_count, halo_sems)
    for copy in incoming[4:]:
        copy.wait()
    over_grp = {}
    for at, step in enumerate(order):
        along_z[step].wait_recv()
        for later in order[at + 2 : at + 3]:
            start_z(later)
        owner = 2 * chip_at(-step) + c
        over_grp[step] = [
            send(
                weights.at[owner, :, columns(k)],
                weights.at[owner, :, columns(k)],
                w_grp_sems,
                (step - 1, offset - 1),
                peer(offset),
            )
            for offset in range(1, blocks)
        ]
    pick_send[...] = picks(table.shape[0], send_idx_ref[...])
    pick_recv[...] = picks(node_count, recv_idx_ref[...])
    joined[:, 2 * width :] = dot_tn(pick_recv[...], fine_ref[...]).astype(BF16)
    upstream_all[...] = cot_edge_ref[...].astype(F32) + dot_tn(pick_recv[...], cot_fine_ref[...])
    for step in order:
        for copy in over_grp[step]:
            copy.wait_recv()
        owner = 2 * chip_at(-step) + c
        between.append(
            send(weights.at[owner], weights.at[owner], w_core_sems, (step,), sibling)
        )
    for copy in halo:
        copy.wait_recv()
    joined[:, width : 2 * width] = dot_tn(pick_send[...], table[...]).astype(BF16)
    for copy in between:
        copy.wait_recv()

    @pl.loop(0, edge_count // EDGE_BLOCK)
    def _(at):
        rows = pl.ds(pl.multiple_of(at * EDGE_BLOCK, EDGE_BLOCK), EDGE_BLOCK)
        first_full = weights[:, :first_rows, :].reshape(patches * first_rows, width)
        second_full = weights[:, first_rows:, :].reshape(patches * second_rows, width)
        pre_act = dot(joined[rows, :], first_full)
        gate_sig = 1.0 / (1.0 + jnp.exp(-pre_act))
        hid = (pre_act * gate_sig).astype(BF16)
        hidden[rows, :] = hid
        outer_proj = dot(hid, second_full)
        centre = outer_proj - row_mean(outer_proj)
        inv_scale = 1.0 / jnp.sqrt(row_mean(centre * centre) + norm_eps)
        normed = centre * inv_scale
        position = lax.broadcasted_iota(jnp.int32, (EDGE_BLOCK, 1), 0)
        per = EDGE_BLOCK // LANES
        bound = counts_ref[at * per]
        for extra in range(1, per):
            bound = jnp.where(
                position < extra * LANES, bound, counts_ref[at * per + extra] + extra * LANES
            )
        live = (position < bound).astype(F32)
        message = live * normed
        message_all[rows, :] = message
        upstream = live * upstream_all[rows, :]
        d_outer = (
            (upstream - row_mean(upstream) - normed * row_mean(upstream * normed)) * inv_scale
        ).astype(BF16)
        d_outer_all[rows, :] = d_outer
        d_hidden = dot_nt(d_outer, second_full)
        d_pre = (d_hidden * gate_sig * (1.0 + pre_act * (1.0 - gate_sig))).astype(BF16)
        d_pre_all[rows, :] = d_pre
        d_send_all[rows, :] = dot_nt(d_pre, first_full[width : 2 * width]).astype(BF16)

    halo_back[...] = dot(
        pick_send[node_count : node_count + halo_count, :], d_send_all[...]
    ).astype(BF16)
    back = exchange(halo_back, returned, 0, back_sems)
    coarse_part = dot(pick_send[node_count + halo_count :, :], d_send_all[...]).astype(BF16)
    second_part = dot_tn(hidden[...], d_outer_all[...]).astype(BF16)
    spare = part_rows - weight_rows - coarse_rows
    for at in range(patches):
        own_coarse = coarse_part[at * coarse_rows : (at + 1) * coarse_rows]
        if spare:
            own_coarse = jnp.concatenate([own_coarse, jnp.zeros((spare, width), BF16)], axis=0)
        parts[at, first_rows:weight_rows, :] = second_part[at * second_rows : (at + 1) * second_rows]
        parts[at, weight_rows:, :] = own_coarse
    turns = list(range(1, chips)) + [0]
    to_core, to_grp, to_z = {}, {}, []
    pair_rows = 2 * first_rows
    by_chip = pair_rows % LANES == 0

    def form(turn):
        chip = chip_at(turn)
        if by_chip:
            span = pl.ds(pl.multiple_of(chip * pair_rows, LANES), pair_rows)
            part = dot_tn(joined[:, span], d_pre_all[...]).astype(BF16)
            parts[2 * chip, :first_rows, :] = part[:first_rows]
            parts[2 * chip + 1, :first_rows, :] = part[first_rows:]
        to_core[turn] = send(
            parts.at[2 * chip + 1 - c], from_core.at[turn], core_sems, (turn,), sibling
        )

    def sum_cores(turn):
        chip = chip_at(turn)
        to_core[turn].wait_recv()
        for block in range(blocks):
            span = slice(block * LANES, (block + 1) * LANES)
            chip_sum[turn, block] = (
                parts[2 * chip + c, :, span].astype(F32) + from_core[turn, :, span].astype(F32)
            ).astype(BF16)
        to_grp[turn] = [
            send(
                chip_sum.at[turn, (k + offset) % blocks],
                from_grp.at[offset - 1, turn],
                grp_sems,
                (turn, offset - 1),
                peer(offset),
            )
            for offset in range(1, blocks)
        ]

    def sum_plane(turn):
        chip = chip_at(turn)
        total = chip_sum[turn, k].astype(F32)
        for offset in range(1, blocks):
            to_grp[turn][offset - 1].wait_recv()
            total = total + from_grp[offset - 1, turn].astype(F32)
        if turn:
            plane_sum[turn - 1] = total.astype(BF16)
            to_z.append(
                send(
                    plane_sum.at[turn - 1],
                    from_z.at[turn - 1],
                    z_sems,
                    (turn - 1,),
                    (a, 2 * chip + c),
                )
            )
        return total

    if not by_chip:
        held = PART_ROWS // first_rows
        for at in range(patches // held):
            part = dot_tn(
                joined[:, at * PART_ROWS : (at + 1) * PART_ROWS], d_pre_all[...]
            ).astype(BF16)
            for place in range(held):
                parts[at * held + place, :first_rows, :] = part[
                    place * first_rows : (place + 1) * first_rows
                ]
    def finish_edges():
        new_edges_ref[...] = (joined[:, :width].astype(F32) + message_all[...]).astype(BF16)
        first_full = weights[:, :first_rows, :].reshape(patches * first_rows, width)
        grad_edges_ref[...] = (
            cot_edge_ref[...].astype(F32) + dot_nt(d_pre_all[...], first_full[:width])
        ).astype(BF16)
        d_recv_all[...] = dot_nt(d_pre_all[...], first_full[2 * width :]).astype(BF16)
        leave(new_edges_ref, new_edges_hbm, 0)
        leave(grad_edges_ref, grad_edges_hbm, 1)

    def finish_nodes():
        fine_msg_ref[...] = dot(pick_recv[...], message_all[...].astype(BF16)).astype(BF16)
        local_grad = dot(pick_send[:node_count, :], d_send_all[...]) + dot(
            pick_recv[...], d_recv_all[...]
        )
        for own in range(4):
            back[own].wait_recv()
        for own in range(4):
            local_grad = local_grad + dot(
                picks(node_count, list_idx_ref[own : own + 1, :]),
                returned[own * list_rows : (own + 1) * list_rows, :],
            )
        grad_fine_ref[...] = local_grad.astype(BF16)
        leave(fine_msg_ref, fine_msg_hbm, 2)
        leave(grad_fine_ref, grad_fine_hbm, 3)

    leaving = []

    def leave(source, target, at):
        copy = pltpu.make_async_copy(source, target, out_sems.at[at])
        copy.start()
        leaving.append(copy)

    stages = ((0, form), (1, sum_cores), (3, sum_plane))
    for at in range(chips + 3):
        for delay, stage in stages:
            if 0 <= at - delay < chips:
                total = stage(turns[at - delay])
        if at == chips:
            finish_edges()
        if at == chips + 1:
            finish_nodes()
    for step in range(1, chips):
        to_z[step - 1].wait_recv()
        total = total + from_z[step - 1].astype(F32)
    whole_sum[...] = total.astype(BF16)
    if far_count > 1:
        to_far = [
            send(
                whole_sum,
                from_far.at[step - 1],
                far_sems,
                (step - 1,),
                ((a + step * blocks) % groups, b),
            )
            for step in range(1, far_count)
        ]
        for step in range(1, far_count):
            to_far[step - 1].wait_recv()
            total = total + from_far[step - 1].astype(F32)
    result[:, columns(k)] = total.astype(BF16)
    shares = [
        send(
            result.at[:, columns(k)],
            result.at[:, columns(k)],
            result_sems,
            (offset - 1,),
            peer(offset),
        )
        for offset in range(1, blocks)
    ]
    for copy in shares:
        copy.wait_recv()
    for copy in leaving:
        copy.wait()
    for copy in pending:
        copy.wait_send()


def finish(first_rows, second_rows, result, *refs):
    sources, targets, shares, sems = refs[:4], refs[4:8], refs[8:11], refs[11]
    copies = [
        pltpu.make_async_copy(source, target, sems.at[at])
        for at, (source, target) in enumerate(zip(sources, targets))
    ]
    for copy in copies:
        copy.start()
    weight_rows = first_rows + second_rows
    shares[0][...] = result[weight_rows:, :].astype(F32)[: shares[0].shape[0]]
    shares[1][...] = result[:first_rows, :].astype(F32)
    shares[2][...] = result[first_rows:weight_rows, :].astype(F32)
    for copy in copies:
        copy.wait()


def on_device(
    groups,
    patches,
    fine_latent,
    edge_latent,
    coarse_latent,
    first_proj,
    second_proj,
    senders,
    receivers,
    block_counts,
    send_rows,
    cot_edges,
    cot_fine,
):
    node_count, width = fine_latent.shape
    edge_count = edge_latent.shape[0]
    halo_count = send_rows.size
    table_rows = node_count + halo_count + coarse_latent.shape[0]
    first_rows = first_proj.shape[0]
    second_rows = second_proj.shape[0]
    coarse_rows = coarse_latent.shape[0] // patches
    weight_rows = first_rows + second_rows
    part_rows = weight_rows + -(-coarse_rows // ROW_TILE) * ROW_TILE
    chips = patches // 2
    blocks = width // LANES
    far = max(groups // blocks - 1, 1)
    vmem = pl.BlockSpec(memory_space=pltpu.VMEM)
    hbm = pl.BlockSpec(memory_space=pltpu.HBM)

    def sems(*shape):
        return pltpu.SemaphoreType.DMA((2,) + shape)

    rows_out = (
        jax.ShapeDtypeStruct((edge_count, width), BF16),
        jax.ShapeDtypeStruct((node_count, width), BF16),
        jax.ShapeDtypeStruct((edge_count, width), BF16),
        jax.ShapeDtypeStruct((node_count, width), BF16),
    )
    *rows, result = pl.pallas_call(
        functools.partial(kernel, groups, patches),
        out_shape=rows_out + (jax.ShapeDtypeStruct((part_rows, width), BF16),),
        in_specs=[hbm] * 11,
        out_specs=(hbm,) * 4 + (vmem,),
        scratch_shapes=[
            pltpu.SMEM(block_counts.shape, jnp.int32),
            pltpu.VMEM((1, edge_count), jnp.int32),
            pltpu.VMEM((1, edge_count), jnp.int32),
            pltpu.VMEM(send_rows.shape, jnp.int32),
            pltpu.VMEM((edge_count, width), BF16),
            pltpu.VMEM((node_count, width), BF16),
            pltpu.VMEM((edge_count, width), BF16),
            pltpu.VMEM((node_count, width), BF16),
            pltpu.VMEM((edge_count, width), BF16),
            pltpu.VMEM((node_count, width), BF16),
            pltpu.VMEM((patches, weight_rows, width), BF16),
            pltpu.VMEM((halo_count, width), BF16),
            pltpu.VMEM((table_rows, width), BF16),
            pltpu.VMEM((table_rows, edge_count), BF16),
            pltpu.VMEM((node_count, edge_count), BF16),
            pltpu.VMEM((edge_count, 3 * width), BF16),
        ]
        + [pltpu.VMEM((edge_count, width), BF16)] * 3
        + [pltpu.VMEM((edge_count, width), F32)] * 2
        + [pltpu.VMEM((edge_count, width), BF16)] * 2
        + [
            pltpu.VMEM((halo_count, width), BF16),
            pltpu.VMEM((halo_count, width), BF16),
            pltpu.VMEM((patches, part_rows, width), BF16),
            pltpu.VMEM((chips, part_rows, width), BF16),
            pltpu.VMEM((chips, blocks, part_rows, LANES), BF16),
            pltpu.VMEM((blocks - 1, chips, part_rows, LANES), BF16),
            pltpu.VMEM((chips - 1, part_rows, LANES), BF16),
            pltpu.VMEM((chips - 1, part_rows, LANES), BF16),
            pltpu.VMEM((part_rows, LANES), BF16),
            pltpu.VMEM((far, part_rows, LANES), BF16),
            pltpu.SemaphoreType.DMA((11,)),
            pltpu.SemaphoreType.DMA((4,)),
            sems(chips - 1),
            sems(chips - 1, blocks - 1),
            sems(chips),
            sems(4),
            sems(4),
            sems(chips),
            sems(chips, blocks - 1),
            sems(chips - 1),
            sems(far),
            sems(blocks - 1),
        ],
        compiler_params=pltpu.CompilerParams(
            collective_id=0, has_side_effects=True, vmem_limit_bytes=62 * 1024 * 1024
        ),
    )(
        block_counts,
        fine_latent,
        edge_latent,
        coarse_latent,
        first_proj,
        second_proj,
        senders.reshape(1, edge_count),
        receivers.reshape(1, edge_count),
        send_rows,
        cot_edges,
        cot_fine,
    )
    shares = tuple(
        jax.ShapeDtypeStruct((count, width), F32)
        for count in (coarse_rows, first_rows, second_rows)
    )
    return pl.pallas_call(
        functools.partial(finish, first_rows, second_rows),
        out_shape=rows_out + shares,
        in_specs=[vmem] * 5,
        out_specs=(hbm,) * 4 + (vmem,) * 3,
        scratch_shapes=[pltpu.SemaphoreType.DMA((4,))],
    )(result, *rows)


def solution(mesh):
    both = P(("grp", "patch"), None)
    flat = P(("grp", "patch"))
    rows = P("patch", None)
    return jax.shard_map(
        functools.partial(on_device, mesh.shape["grp"], mesh.shape["patch"]),
        mesh=mesh,
        in_specs=(both, both, P(), rows, rows, flat, flat, flat, both, both, both),
        out_specs=(both, both, both, both, rows, rows, rows),
        check_vma=False,
    )
```
